256 devices in a mesh: src: 8 (over z), tgt: 32 (over y, x, core).
Axes of the slice: x: 4, y: 4, z: 8, core: 2. Of those that a mesh axis runs over, the one named last changes fastest.
Arguments:
- src_cells: bfloat16 [64, 131072], P(None, 'src'), may hold values from -6 to 6
- tgt_cells: bfloat16 [64, 131072], P(None, 'tgt'), may hold values from -2 to 2
- src_logmass: float32 [131072], P('src'), may hold values from -1 to 1
- tgt_logmass: float32 [131072], P('tgt'), may hold values from -1 to 1
- init_potential: float32 [131072], P('tgt'), may hold values from -1 to 60
- pattern: int32 [256, 256], P('src', 'tgt'), may hold values from 0 to 1, as said below
Outputs:
- src_potential: float32 [131072], P('src')
- tgt_potential: float32 [131072], P('tgt')
The draws below stay inside these ranges and needn't reach their ends.
Inputs may be any that keep to these rules, and one draw needn't show every extreme that they name: pattern[i, j] = 1 marks source block i (cells i * 512 to (i + 1) * 512 - 1) and target block j as an active pair, 0 an inactive one; pattern[i, i mod 256] = 1 for every source block i.
All inputs are finite; a program needn't handle non-finite values.
Results may differ from the reference program's by a relative error of at most 0.0005.
Values sent between devices are 32-bit elements; how exact they have to be, the bound alone decides.
No kernel may reach another device: no remote copies, remote signals or barrier semaphores. Data moves between devices by JAX's collectives and lax.ppermute only.
A program may use at most 64 MiB of HBM per device.

```python
import jax
import jax.numpy as jnp
from jax import lax

DIM = 64
BLOCK = 512
SWEEPS = 2
NSB = 256
NTB = 256
NS = 131072
NT = 131072


def target_table(key):
    subkeys = jax.random.split(key, 1)
    normal_part = jax.random.truncated_normal(subkeys[0], -4.0, 4.0, (DIM, NT), jnp.float32) * 0.25
    bulk_part = normal_part
    position = jnp.arange(NT, dtype=jnp.int32) % BLOCK
    second = position == 1
    return jnp.where(second[None, :], bulk_part, bulk_part)


def draw_tgt_cells(key, part):
    table_cells = target_table(key)
    return table_cells.astype(jnp.bfloat16)


def draw_src_cells(key, part):
    key = jax.random.fold_in(key, 7)
    subkeys = jax.random.split(key, 1)
    bulk_part = jax.random.truncated_normal(subkeys[0], -4.0, 4.0, (DIM, NS), jnp.float32) * 0.25
    return bulk_part.astype(jnp.bfloat16)


def draw_init_potential(key, part):
    key = jax.random.fold_in(key, 11)
    subkeys = jax.random.split(key, 1)
    bulk_part = jax.random.uniform(subkeys[0], (NT,), jnp.float32, -1.0, 1.0)
    return bulk_part


def draw_pattern(key, part):
    key = jax.random.fold_in(key, 5)
    subkeys = jax.random.split(key, 2)
    levels = jax.random.randint(subkeys[0], (NTB,), 0, 5)
    limits = jnp.left_shift(jnp.ones_like(levels), levels)
    roll_values = jax.random.randint(subkeys[1], (NSB, NTB), 0, 64)
    row_home = jnp.arange(NSB, dtype=jnp.int32) % NTB
    diagonal = row_home[:, None] == jnp.arange(NTB, dtype=jnp.int32)[None, :]
    return jnp.where(diagonal | (roll_values < limits[None, :]), 1, 0).astype(jnp.int32)


def level_of(rng, extent, pieces, least, largest):
    def one(axis_at, parts):
        steps = jax.random.uniform(jax.random.fold_in(jax.random.fold_in(rng, 6), axis_at), (parts,), jnp.float32, least / len(pieces), largest / len(pieces))
        return jnp.repeat(jnp.exp(steps), extent[axis_at] // parts).reshape((-1,) + (1,) * (len(extent) - axis_at - 1))

    loudness = one(*pieces[0])
    for cut in pieces[1:]:
        loudness = loudness * one(*cut)
    return loudness


def setup_inputs(seed: int = 0) -> dict:
    key_of = jax.random.split(jax.random.key(seed), 7)
    src_cells = draw_src_cells(jax.random.fold_in(key_of[6], 71), 0)
    tgt_cells = draw_tgt_cells(jax.random.fold_in(key_of[6], 71), 0)
    src_logmass = jnp.clip(jax.random.uniform(key_of[2], (NS,), jnp.float32, -1.0, 1.0) * level_of(key_of[2], (NS,), ((0, 8),), -0.4, 0.0), -1.0, 1.0)
    tgt_logmass = jnp.clip(jax.random.uniform(key_of[3], (NT,), jnp.float32, -1.0, 1.0) * level_of(key_of[3], (NT,), ((0, 32),), -0.4, 0.0), -1.0, 1.0)
    init_potential = draw_init_potential(jax.random.fold_in(key_of[6], 71), 0)
    pattern = draw_pattern(jax.random.fold_in(key_of[6], 71), 0)
    return dict(src_cells=src_cells, tgt_cells=tgt_cells, src_logmass=src_logmass, tgt_logmass=tgt_logmass, init_potential=init_potential, pattern=pattern)


entropy = 0.5
lowest = -1.0e30


def block_lse(row_cells, col_cells, row_sq, col_sq, col_pot, pair_mask):
    group_size = 32
    feature_dim = row_cells.shape[0]
    row_span, col_span = pair_mask.shape
    block_width = row_sq.shape[1]
    row_blocks = row_cells.astype(jnp.float32).reshape(feature_dim, row_span, block_width)
    col_blocks = col_cells.astype(jnp.float32).reshape(feature_dim, col_span, block_width)
    flat_mask = pair_mask.reshape(-1).astype(jnp.int32)
    slot_count = flat_mask.shape[0]
    slot_ids = jnp.arange(slot_count, dtype=jnp.int32)
    active_order = jnp.argsort((1 - flat_mask) * slot_count + slot_ids).astype(jnp.int32)
    active_order = jnp.concatenate([active_order, jnp.zeros((group_size,), jnp.int32)])
    active_count = jnp.sum(flat_mask).astype(jnp.int32)
    rounds = (active_count + group_size - 1) // group_size

    def advance(round_index, carry):
        running_max, total_sum = carry
        picked = lax.dynamic_slice_in_dim(active_order, round_index * group_size, group_size)
        live_slot = (round_index * group_size + jnp.arange(group_size, dtype=jnp.int32)) < active_count
        row_pick = picked // col_span
        col_pick = picked % col_span
        row_tiles = jnp.take(row_blocks, row_pick, axis=1)
        col_tiles = jnp.take(col_blocks, col_pick, axis=1)
        inner_tiles = jnp.einsum("dgr,dgc->grc", row_tiles, col_tiles)
        tile_cost = row_sq[row_pick][:, :, None] + col_sq[col_pick][:, None, :] - 2.0 * inner_tiles
        scores = (col_pot[col_pick][:, None, :] - tile_cost) / entropy
        row_top = jnp.where(live_slot[:, None], jnp.max(scores, axis=2), lowest)
        new_max = running_max.at[row_pick].max(row_top)
        tile_terms = jnp.sum(jnp.exp(scores - new_max[row_pick][:, :, None]), axis=2)
        tile_terms = jnp.where(live_slot[:, None], tile_terms, 0.0)
        rescaled = total_sum * jnp.exp(running_max - new_max)
        return new_max, rescaled.at[row_pick].add(tile_terms)

    start_max = jnp.full((row_span, block_width), lowest, jnp.float32)
    start_sum = jnp.zeros((row_span, block_width), jnp.float32)
    return lax.fori_loop(0, rounds, advance, (start_max, start_sum))


def finish(logmass, row_top, row_total):
    return entropy * logmass - entropy * (row_top + jnp.log(row_total))


def reference(src_cells, tgt_cells, src_logmass, tgt_logmass, init_potential, pattern):
    src_sq = jnp.sum(jnp.square(src_cells.astype(jnp.float32)), axis=0).reshape(-1, BLOCK)
    tgt_sq = jnp.sum(jnp.square(tgt_cells.astype(jnp.float32)), axis=0).reshape(-1, BLOCK)
    tgt_pot = init_potential
    src_pot = jnp.zeros_like(src_logmass)
    for sweep_index in range(SWEEPS):
        row_top, row_total = block_lse(src_cells, tgt_cells, src_sq, tgt_sq, tgt_pot.reshape(-1, BLOCK), pattern)
        src_pot = finish(src_logmass, row_top.reshape(-1), row_total.reshape(-1))
        col_top, col_total = block_lse(tgt_cells, src_cells, tgt_sq, src_sq, src_pot.reshape(-1, BLOCK), pattern.T)
        tgt_pot = finish(tgt_logmass, col_top.reshape(-1), col_total.reshape(-1))
    return src_pot, tgt_pot
```

```python
import functools

import jax
import jax.numpy as jnp
from jax import lax
from jax.experimental import pallas as pl
from jax.experimental.pallas import tpu as pltpu
from jax.sharding import PartitionSpec as P

BLOCK = 512
SWEEPS = 2
DEPTH = 128
ENTROPY = 0.5
LOWEST = -1e30
GROUP = 8
VMEM_LIMIT = 48 << 20


def list_pairs(pattern_ref, list_ref):
    rows, cols = pattern_ref.shape

    def visit(row, count):
        for col in range(cols):
            list_ref[count] = row * cols + col
            count = count + pattern_ref[row, col]
        return count

    count = lax.fori_loop(0, rows, visit, jnp.int32(0))
    for extra in range(GROUP):
        list_ref[count + extra] = rows * cols
    return count


def pieces(values):
    high = values.astype(jnp.bfloat16).astype(jnp.float32)
    rest = values - high
    middle = rest.astype(jnp.bfloat16).astype(jnp.float32)
    low = (rest - middle).astype(jnp.bfloat16).astype(jnp.float32)
    return high, middle, low


def piece_rows(parts, row_count):
    at = lax.broadcasted_iota(jnp.int32, (row_count, BLOCK), 0)
    out = jnp.zeros((row_count, BLOCK), jnp.float32)
    for index, part in enumerate(parts):
        out = jnp.where(at == index, part, out)
    return out


def fill_src(src_ref, wide_ref, rows_of):
    wide_ref[0:64, :] = src_ref[...] * jnp.bfloat16(4)
    wide_ref[80:DEPTH, :] = jnp.zeros((DEPTH - 80, wide_ref.shape[1]), jnp.bfloat16)
    for block in range(wide_ref.shape[1] // BLOCK):
        wide_ref[64:80, block * BLOCK : (block + 1) * BLOCK] = rows_of(block).astype(jnp.bfloat16)


def fill_tgt(tgt_ref, tall_ref, rows_of):
    for block in range(tgt_ref.shape[1] // BLOCK):
        cells = tgt_ref[:, block * BLOCK : (block + 1) * BLOCK].astype(jnp.float32)
        whole = jnp.concatenate(
            [cells, rows_of(block), jnp.zeros((DEPTH - 80, BLOCK), jnp.float32)], axis=0
        )
        tall_ref[block * BLOCK : (block + 1) * BLOCK, :] = whole.T.astype(jnp.bfloat16)


def one_rows(block):
    at = lax.broadcasted_iota(jnp.int32, (16, BLOCK), 0)
    return jnp.where(at < 3, 1.0, 0.0).astype(jnp.float32)


def shift_of(potential, reach):
    tops = jnp.max(potential, axis=1, keepdims=True)
    shift = jnp.max(tops)
    spread = shift - jnp.min(tops)
    safe = jnp.logical_and(reach <= 70.0, reach + spread <= 80.0)
    return shift, safe


def run_pairs(count, list_ref, visit):
    def turn(width, base):
        def body(step, carry):
            for at in range(width):
                visit(list_ref[base + step * width + at])
            return carry

        return body

    full = count // GROUP
    lax.fori_loop(0, full, turn(GROUP, 0), 0)
    lax.fori_loop(0, (count - full * GROUP + 1) // 2, turn(2, full * GROUP), 0)


def run_pairs_singly(count, list_ref, visit):
    def body(step, carry):
        visit(list_ref[step])
        return carry

    lax.fori_loop(0, count, body, 0)


def tile_of(tall_ref, wide_ref, pair, start, size):
    cols = 8
    src_block = lax.rem(lax.div(pair, cols), wide_ref.shape[1] // BLOCK)
    tgt_block = lax.rem(pair, cols)
    left = tall_ref[pl.ds(pl.multiple_of(tgt_block * BLOCK + start, size), size), :]
    right = wide_ref[:, pl.ds(pl.multiple_of(src_block * BLOCK, BLOCK), BLOCK)]
    return jnp.dot(left, right, preferred_element_type=jnp.float32)


def src_sums(count, safe, shift, list_ref, tall_ref, wide_ref, sum_ref, top_ref, out_ref):
    sum_ref[...] = jnp.zeros_like(sum_ref)
    blocks = out_ref.shape[0]

    @pl.when(safe)
    def _():
        def visit(pair):
            tile = jnp.exp(tile_of(tall_ref, wide_ref, pair, 0, BLOCK))
            sum_ref[lax.div(pair, 8)] += tile.reshape(-1, 8, BLOCK).sum(0)

        run_pairs(count, list_ref, visit)
        total = sum_ref[0:blocks].sum(1)
        out_ref[...] = jnp.where(
            total > 0.0, jnp.log(jnp.where(total > 0.0, total, 1.0)) + shift, LOWEST
        )

    @pl.when(jnp.logical_not(safe))
    def _():
        top_ref[...] = jnp.full_like(top_ref, LOWEST)

        def visit(pair):
            at = lax.div(pair, 8)

            def chunk(index, carry):
                tile = tile_of(tall_ref, wide_ref, pair, index * 128, 128).reshape(-1, 8, BLOCK)
                old = top_ref[at]
                new = jnp.maximum(old, tile.max(0))
                sum_ref[at] = sum_ref[at] * jnp.exp(old - new) + jnp.exp(tile - new[None]).sum(0)
                top_ref[at] = new
                return carry

            lax.fori_loop(0, BLOCK // 128, chunk, 0)

        run_pairs_singly(count, list_ref, visit)
        slots = top_ref[0:blocks]
        top = slots.max(1, keepdims=True)
        total = (sum_ref[0:blocks] * jnp.exp(slots - top)).sum(1)
        out_ref[...] = jnp.where(
            total > 0.0, jnp.log(jnp.where(total > 0.0, total, 1.0)) + top[:, 0] + shift, LOWEST
        )


def fold_lanes(tile, fold):
    out = tile[:, 0:128]
    for start in range(128, tile.shape[1], 128):
        out = fold(out, tile[:, start : start + 128])
    return out


def tgt_sums(count, safe, shift, list_ref, tall_ref, wide_ref, sum_ref, top_ref, out_ref):
    sum_ref[...] = jnp.zeros_like(sum_ref)
    blocks = out_ref.shape[0]

    def finish_block(block, total, top):
        out_ref[block : block + 1, :] = jnp.where(
            total > 0.0, jnp.log(jnp.where(total > 0.0, total, 1.0)) + top + shift, LOWEST
        )

    @pl.when(safe)
    def _():
        def visit(pair):
            at = jnp.where(pair < 32 * 8, lax.rem(pair, 8), 8)
            for start in range(0, BLOCK, 128):
                tile = jnp.exp(tile_of(tall_ref, wide_ref, pair, start, 128))
                sum_ref[at, start : start + 128, :] += fold_lanes(tile, jnp.add)

        run_pairs(count, list_ref, visit)
        for block in range(blocks):
            total = sum_ref[block].T.sum(0, keepdims=True)
            finish_block(block, total, 0.0)

    @pl.when(jnp.logical_not(safe))
    def _():
        top_ref[...] = jnp.full_like(top_ref, LOWEST)

        def visit(pair):
            at = lax.rem(pair, 8)

            def chunk(index, carry):
                tile = tile_of(tall_ref, wide_ref, pair, index * 128, 128)
                rows = pl.ds(pl.multiple_of(index * 128, 128), 128)
                old = top_ref[at, rows, :]
                new = jnp.maximum(old, fold_lanes(tile, jnp.maximum))
                wide_new = jnp.concatenate([new] * (BLOCK // 128), axis=1)
                sum_ref[at, rows, :] = sum_ref[at, rows, :] * jnp.exp(old - new) + fold_lanes(
                    jnp.exp(tile - wide_new), jnp.add
                )
                top_ref[at, rows, :] = new
                return carry

            lax.fori_loop(0, BLOCK // 128, chunk, 0)

        run_pairs_singly(count, list_ref, visit)
        for block in range(blocks):
            slots = top_ref[block].T
            top = slots.max(0, keepdims=True)
            total = (sum_ref[block].T * jnp.exp(slots - top)).sum(0, keepdims=True)
            finish_block(block, total, top)


def square_rows(cells_ref, out_ref):
    for block in range(out_ref.shape[0]):
        cells = cells_ref[:, block * BLOCK : (block + 1) * BLOCK].astype(jnp.float32)
        out_ref[block : block + 1, :] = jnp.sum(cells * cells, axis=0, keepdims=True)


def first_src_kernel(
    pattern_ref, src_ref, tgt_ref, pot_ref, out_ref, src_sq_ref, tgt_sq_ref, reach_ref,
    list_ref, tall_ref, wide_ref, sum_ref, top_ref,
):
    count = list_pairs(pattern_ref, list_ref)
    square_rows(src_ref, src_sq_ref)
    square_rows(tgt_ref, tgt_sq_ref)
    reach = 4.0 * jnp.sqrt(jnp.max(src_sq_ref[...], keepdims=True)) * jnp.sqrt(
        jnp.max(tgt_sq_ref[...], keepdims=True)
    )
    reach_ref[...] = jnp.broadcast_to(reach, reach_ref.shape)
    potential = 2.0 * (pot_ref[...] - tgt_sq_ref[...])
    shift, safe = shift_of(potential, jnp.max(reach))
    parts = pieces(potential - shift)
    fill_tgt(tgt_ref, tall_ref, lambda at: piece_rows([p[at : at + 1] for p in parts], 16))
    fill_src(src_ref, wide_ref, one_rows)
    src_sums(count, safe, shift, list_ref, tall_ref, wide_ref, sum_ref, top_ref, out_ref)


def src_kernel(
    pattern_ref, src_ref, tgt_ref, gathered_ref, mass_ref, reach_ref, out_ref,
    list_ref, tall_ref, wide_ref, sum_ref, top_ref,
):
    count = list_pairs(pattern_ref, list_ref)
    gathered = gathered_ref[...]
    top = gathered.max(0)
    logs = top + jnp.log(jnp.exp(gathered - top[None]).sum(0))
    potential = mass_ref[...] - logs
    shift, safe = shift_of(potential, jnp.max(reach_ref[...]))
    parts = pieces(potential - shift)
    fill_tgt(tgt_ref, tall_ref, lambda at: piece_rows([p[at : at + 1] for p in parts], 16))
    fill_src(src_ref, wide_ref, one_rows)
    src_sums(count, safe, shift, list_ref, tall_ref, wide_ref, sum_ref, top_ref, out_ref)


def tgt_kernel(
    pattern_ref, src_ref, tgt_ref, logs_ref, mass_ref, reach_ref, out_ref,
    list_ref, tall_ref, wide_ref, sum_ref, top_ref,
):
    count = list_pairs(pattern_ref, list_ref)
    potential = mass_ref[...] - logs_ref[...]
    shift, safe = shift_of(potential, jnp.max(reach_ref[...]))
    parts = pieces(potential - shift)
    fill_tgt(tgt_ref, tall_ref, one_rows)
    fill_src(src_ref, wide_ref, lambda at: piece_rows([p[at : at + 1] for p in parts], 16))
    tgt_sums(count, safe, shift, list_ref, tall_ref, wide_ref, sum_ref, top_ref, out_ref)


def call(kernel, args, outs, src_count, tgt_count, sums):
    vmem = pl.BlockSpec(memory_space=pltpu.VMEM)
    smem = pl.BlockSpec(memory_space=pltpu.SMEM)
    slots = src_count // BLOCK * (tgt_count // BLOCK)
    return pl.pallas_call(
        kernel,
        out_shape=[jax.ShapeDtypeStruct(shape, jnp.float32) for shape in outs],
        in_specs=[smem] + [vmem] * (len(args) - 1),
        out_specs=[vmem] * len(outs),
        scratch_shapes=[
            pltpu.SMEM((slots + GROUP,), jnp.int32),
            pltpu.VMEM((tgt_count, DEPTH), jnp.bfloat16),
            pltpu.VMEM((DEPTH, src_count), jnp.bfloat16),
            pltpu.VMEM(sums, jnp.float32),
            pltpu.VMEM(sums, jnp.float32),
        ],
        compiler_params=pltpu.CompilerParams(vmem_limit_bytes=VMEM_LIMIT),
    )(*args)


def combine(one, other):
    top = jnp.maximum(one, other)
    return top + jnp.log(1.0 + jnp.exp(-jnp.abs(one - other)))


def over_tgt(logs):
    size = lax.axis_size("tgt")
    for mask in (1, 2, 6, 8, 24):
        other = lax.ppermute(logs, "tgt", [(at, at ^ mask) for at in range(size)])
        logs = combine(logs, other)
    return logs


def over_src(logs):
    size = lax.axis_size("src")
    return lax.all_to_all(jnp.broadcast_to(logs[None], (size,) + logs.shape), "src", 0, 0)


def local(src_cells, tgt_cells, src_logmass, tgt_logmass, init_potential, pattern):
    src_count, tgt_count = src_cells.shape[1], tgt_cells.shape[1]
    src_shape = (src_count // BLOCK, BLOCK)
    tgt_shape = (tgt_count // BLOCK, BLOCK)
    src_mass = src_logmass.reshape(src_shape)
    tgt_mass = tgt_logmass.reshape(tgt_shape)
    src_sums_shape = (src_shape[0] + 1, 8, BLOCK)
    tgt_sums_shape = (tgt_shape[0] + 1, BLOCK, 128)
    cells = [pattern, src_cells, tgt_cells]
    sizes = (src_count, tgt_count)

    logs, src_sq, tgt_sq, reach = call(
        first_src_kernel, cells + [init_potential.reshape(tgt_shape)],
        [src_shape, src_shape, tgt_shape, (8, 128)], *sizes, src_sums_shape,
    )
    for sweep in range(SWEEPS):
        if sweep:
            (logs,) = call(
                src_kernel, cells + [gathered, tgt_mass, reach], [src_shape], *sizes, src_sums_shape
            )
        src_logs = over_tgt(logs)
        (logs,) = call(
            tgt_kernel, cells + [src_logs, src_mass, reach], [tgt_shape], *sizes, tgt_sums_shape
        )
        gathered = over_src(logs)
    top = gathered.max(0)
    tgt_logs = top + jnp.log(jnp.exp(gathered - top[None]).sum(0))
    src_pot = src_sq + ENTROPY * (src_mass - src_logs)
    tgt_pot = tgt_sq + ENTROPY * (tgt_mass - tgt_logs)
    return src_pot.reshape(-1), tgt_pot.reshape(-1)


def solution(mesh):
    return jax.shard_map(
        local,
        mesh=mesh,
        in_specs=(P(None, "src"), P(None, "tgt"), P("src"), P("tgt"), P("tgt"), P("src", "tgt")),
        out_specs=(P("src"), P("tgt")),
        check_vma=False,
    )
```

```python
import jax
import jax.numpy as jnp
from jax import lax
from jax.experimental import pallas as pl
from jax.experimental.pallas import tpu as pltpu
from jax.sharding import PartitionSpec as P

BLOCK = 512
LANES = 128
PARTS = BLOCK // LANES
SWEEPS = 2
ENTROPY = 0.5
LOWEST = -1e30
GROUP = 8
VMEM_LIMIT = 40 << 20


def list_pairs(pattern_ref, list_ref):
    cols, rows = pattern_ref.shape
    count = jnp.int32(0)
    for row in range(rows):
        for col in range(cols):
            list_ref[count] = row * cols + col
            count = count + pattern_ref[col, row]
    for extra in range(GROUP):
        list_ref[count + extra] = rows * cols
    list_ref[rows * cols + GROUP] = count


def blocks_of(ref):
    rows = ref.shape[0] // PARTS
    return jnp.concatenate([ref[pl.ds(part, rows, stride=PARTS), :] for part in range(PARTS)], axis=1)


def store_blocks(ref, values):
    rows = values.shape[0]
    for part in range(PARTS):
        ref[pl.ds(part, rows, stride=PARTS), :] = values[:, part * LANES : (part + 1) * LANES]


def factors(potential, reach):
    shift = jnp.max(potential)
    extent = shift - jnp.min(potential)
    safe = jnp.logical_and(reach <= 70.0, reach + extent <= 80.0)
    below = potential - shift
    return jnp.where(safe, jnp.exp(below), below), shift, safe


def log_or_lowest(total, top):
    some = total > 0.0
    return jnp.where(some, jnp.log(jnp.where(some, total, 1.0)) + top, LOWEST)


def run_pairs(list_ref, visit):
    count = list_ref[list_ref.shape[0] - 1]

    def turn(width, base):
        def body(step, carry):
            for at in range(width):
                visit(list_ref[base + step * width + at])
            return carry

        return body

    full = lax.div(count, GROUP)
    lax.fori_loop(0, full, turn(GROUP, 0), 0)
    lax.fori_loop(0, lax.div(count - full * GROUP + 1, 2), turn(2, full * GROUP), 0)


def run_pairs_singly(list_ref, visit):
    def body(step, carry):
        visit(list_ref[step])
        return carry

    lax.fori_loop(0, list_ref[list_ref.shape[0] - 1], body, 0)


def place(pair, rows, cols):
    return lax.rem(lax.div(pair, cols), rows), lax.rem(pair, cols)


def tile_of(tall_ref, src_ref, src_block, tgt_block, start=0, size=BLOCK):
    left = tall_ref[pl.ds(pl.multiple_of(tgt_block * BLOCK + start, size), size), :]
    right = src_ref[:, pl.ds(pl.multiple_of(src_block * BLOCK, BLOCK), BLOCK)]
    return jnp.dot(left, right, preferred_element_type=jnp.float32)


def lane_part(values, part):
    return values[:, part * LANES : (part + 1) * LANES]


def fold_lanes(values, fold):
    out = lane_part(values, 0)
    for part in range(1, PARTS):
        out = fold(out, lane_part(values, part))
    return out


def spread_down(weights, spread_ref):
    for row in range(weights.shape[0]):
        down = jnp.broadcast_to(weights[row : row + 1, :], (LANES, LANES)).T
        spread_ref[row * LANES : (row + 1) * LANES, :] = down


def src_sums(potential, reach, list_ref, tall_ref, src_ref, spread_ref, sum_ref, top_ref, out_ref):
    rows, cols = src_ref.shape[1] // BLOCK, tall_ref.shape[0] // BLOCK
    weights, shift, safe = factors(potential, reach)
    spread_down(weights, spread_ref)
    sum_ref[...] = jnp.zeros_like(sum_ref)

    @pl.when(safe)
    def _():
        def visit(pair):
            src_block, tgt_block = place(pair, rows, cols)
            tile = jnp.exp(tile_of(tall_ref, src_ref, src_block, tgt_block))
            down = spread_ref[pl.ds(pl.multiple_of(tgt_block * BLOCK, BLOCK), BLOCK), :]
            sums = [
                (lane_part(tile, part) * down).reshape(-1, 8, LANES).sum(0) for part in range(PARTS)
            ]
            sum_ref[lax.div(pair, cols)] += jnp.concatenate(sums, axis=1)

        run_pairs(list_ref, visit)
        store_blocks(out_ref, log_or_lowest(sum_ref[0:rows].sum(1), shift))

    @pl.when(jnp.logical_not(safe))
    def _():
        top_ref[...] = jnp.full_like(top_ref, LOWEST)

        def visit(pair):
            src_block, tgt_block = place(pair, rows, cols)

            def chunk(index, carry):
                start = pl.multiple_of(index * LANES, LANES)
                down = spread_ref[pl.ds(pl.multiple_of(tgt_block * BLOCK + start, LANES), LANES), :]
                tile = tile_of(tall_ref, src_ref, src_block, tgt_block, start, LANES)
                tile = (tile + jnp.concatenate([down] * PARTS, axis=1)).reshape(-1, 8, BLOCK)
                old = top_ref[src_block]
                new = jnp.maximum(old, tile.max(0))
                more = jnp.exp(tile - new[None]).sum(0)
                sum_ref[src_block] = sum_ref[src_block] * jnp.exp(old - new) + more
                top_ref[src_block] = new
                return carry

            lax.fori_loop(0, PARTS, chunk, 0)

        run_pairs_singly(list_ref, visit)
        slots = top_ref[0:rows]
        top = slots.max(1, keepdims=True)
        total = (sum_ref[0:rows] * jnp.exp(slots - top)).sum(1)
        store_blocks(out_ref, log_or_lowest(total, top[:, 0] + shift))


def tgt_sums(potential, reach, list_ref, tall_ref, src_ref, weight_ref, sum_ref, top_ref, out_ref):
    rows, cols = src_ref.shape[1] // BLOCK, tall_ref.shape[0] // BLOCK
    weights, shift, safe = factors(potential, reach)
    weight_ref[...] = weights
    sum_ref[...] = jnp.zeros_like(sum_ref)

    def store(block, total, top):
        values = log_or_lowest(total, top)
        for part in range(PARTS):
            at = block * PARTS + part
            out_ref[0, at : at + 1, :] = lane_part(values, part)

    @pl.when(safe)
    def _():
        def visit(pair):
            src_block, tgt_block = place(pair, rows, cols)
            at = jnp.where(pair < rows * cols, tgt_block, cols)
            tile = jnp.exp(tile_of(tall_ref, src_ref, src_block, tgt_block))
            sum_ref[at] += fold_lanes(tile * weight_ref[pl.ds(src_block, 1), :], jnp.add)

        run_pairs(list_ref, visit)
        for block in range(cols):
            store(block, sum_ref[block].T.sum(0, keepdims=True), shift)

    @pl.when(jnp.logical_not(safe))
    def _():
        top_ref[...] = jnp.full_like(top_ref, LOWEST)

        def visit(pair):
            src_block, tgt_block = place(pair, rows, cols)
            right = weight_ref[pl.ds(src_block, 1), :]

            def chunk(index, carry):
                start = pl.multiple_of(index * LANES, LANES)
                tile = tile_of(tall_ref, src_ref, src_block, tgt_block, start, LANES) + right
                at = (tgt_block, pl.ds(start, LANES), slice(None))
                old = top_ref[at]
                new = jnp.maximum(old, fold_lanes(tile, jnp.maximum))
                more = fold_lanes(jnp.exp(tile - jnp.concatenate([new] * PARTS, axis=1)), jnp.add)
                sum_ref[at] = sum_ref[at] * jnp.exp(old - new) + more
                top_ref[at] = new
                return carry

            lax.fori_loop(0, PARTS, chunk, 0)

        run_pairs_singly(list_ref, visit)
        for block in range(cols):
            slots = top_ref[block].T
            top = slots.max(0, keepdims=True)
            total = (sum_ref[block].T * jnp.exp(slots - top)).sum(0, keepdims=True)
            store(block, total, top + shift)

    for copy in range(1, out_ref.shape[0]):
        out_ref[copy] = out_ref[0]


def store_squares(cells_ref, out_ref):
    for block in range(cells_ref.shape[1] // BLOCK):
        cells = cells_ref[:, block * BLOCK : (block + 1) * BLOCK].astype(jnp.float32)
        squares = jnp.sum(cells * cells, axis=0, keepdims=True)
        for part in range(PARTS):
            at = block * PARTS + part
            out_ref[at : at + 1, :] = lane_part(squares, part)


def first_src_kernel(
    pattern_hbm, src_hbm, tgt_hbm, pot_hbm,
    out_ref, src_ref, src_sq_ref, tgt_sq_ref, reach_ref, tall_ref, list_ref,
    pattern_ref, tgt_ref, pot_ref, sems, spread_ref, sum_ref, top_ref,
):
    pattern_copy, tgt_copy, pot_copy, src_copy = copies = [
        pltpu.make_async_copy(source, target, sems.at[at])
        for at, (source, target) in enumerate(
            [(pattern_hbm, pattern_ref), (tgt_hbm, tgt_ref), (pot_hbm, pot_ref), (src_hbm, src_ref)]
        )
    ]
    for copy in copies:
        copy.start()
    pattern_copy.wait()
    list_pairs(pattern_ref, list_ref)
    tgt_copy.wait()
    for block in range(tgt_ref.shape[1] // BLOCK):
        cells = tgt_ref[:, block * BLOCK : (block + 1) * BLOCK].astype(jnp.float32) * 4.0
        tall_ref[block * BLOCK : (block + 1) * BLOCK, :] = cells.T.astype(jnp.bfloat16)
    store_squares(tgt_ref, tgt_sq_ref)
    pot_copy.wait()
    src_copy.wait()
    store_squares(src_ref, src_sq_ref)
    reach = 4.0 * jnp.sqrt(jnp.max(src_sq_ref[...], keepdims=True)) * jnp.sqrt(
        jnp.max(tgt_sq_ref[...], keepdims=True)
    )
    reach_ref[...] = jnp.broadcast_to(reach, reach_ref.shape)
    potential = 2.0 * (pot_ref[...] - tgt_sq_ref[...])
    src_sums(
        potential, jnp.max(reach), list_ref, tall_ref, src_ref, spread_ref, sum_ref, top_ref, out_ref
    )


def src_kernel(
    list_ref, src_ref, tall_ref, gathered_ref, mass_ref, reach_ref,
    out_ref,
    spread_ref, sum_ref, top_ref,
):
    gathered = gathered_ref[...]
    top = gathered.max(0)
    potential = mass_ref[...] - (top + jnp.log(jnp.exp(gathered - top[None]).sum(0)))
    src_sums(
        potential, jnp.max(reach_ref[...]), list_ref, tall_ref, src_ref, spread_ref, sum_ref, top_ref,
        out_ref,
    )


def tgt_kernel(
    list_ref, src_ref, tall_ref, logs_ref, mass_ref, reach_ref,
    out_ref,
    weight_ref, sum_ref, top_ref,
):
    potential = blocks_of(mass_ref) - blocks_of(logs_ref)
    tgt_sums(
        potential, jnp.max(reach_ref[...]), list_ref, tall_ref, src_ref, weight_ref, sum_ref, top_ref,
        out_ref,
    )


def last_tgt_kernel(
    list_ref, src_ref, tall_ref, logs_ref, mass_ref, reach_ref, src_sq_ref,
    out_ref, src_pot_hbm,
    weight_ref, sum_ref, top_ref, src_pot_ref, sem,
):
    src_pot_ref[...] = src_sq_ref[...] + ENTROPY * (mass_ref[...] - logs_ref[...])
    copy = pltpu.make_async_copy(src_pot_ref, src_pot_hbm, sem)
    copy.start()
    tgt_kernel(
        list_ref, src_ref, tall_ref, logs_ref, mass_ref, reach_ref, out_ref, weight_ref, sum_ref, top_ref
    )
    copy.wait()


def call(kernel, args, in_spaces, outs, out_spaces, scratch, name):
    return pl.pallas_call(
        kernel,
        out_shape=outs,
        in_specs=[pl.BlockSpec(memory_space=space) for space in in_spaces],
        out_specs=[pl.BlockSpec(memory_space=space) for space in out_spaces],
        scratch_shapes=scratch,
        compiler_params=pltpu.CompilerParams(vmem_limit_bytes=VMEM_LIMIT),
        name=name,
    )(*args)


def floats(*shape):
    return jax.ShapeDtypeStruct(shape, jnp.float32)


def combine(one, other):
    top = jnp.maximum(one, other)
    return top + jnp.log(1.0 + jnp.exp(-jnp.abs(one - other)))


def over_tgt(logs):
    size = lax.axis_size("tgt")

    def from_peer(values, mask):
        return lax.ppermute(values, "tgt", [(at, at ^ mask) for at in range(size)])

    logs = combine(logs, from_peer(logs, 1))
    for stage in (2, 8):
        one, two, three = [from_peer(logs, stage * mask) for mask in (1, 2, 3)]
        top = jnp.maximum(jnp.maximum(logs, one), jnp.maximum(two, three))
        near = jnp.exp(logs - top) + jnp.exp(one - top)
        far = jnp.exp(two - top) + jnp.exp(three - top)
        logs = top + jnp.log(near + far)
    return logs


def local(src_cells, tgt_cells, src_logmass, tgt_logmass, init_potential, pattern):
    copies = lax.axis_size("src")
    depth, src_count = src_cells.shape
    tgt_count = tgt_cells.shape[1]
    rows, cols = pattern.shape
    src_shape = (src_count // LANES, LANES)
    tgt_shape = (tgt_count // LANES, LANES)
    src_mass = src_logmass.reshape(src_shape)
    tgt_mass = tgt_logmass.reshape(tgt_shape)
    vmem, smem, hbm = pltpu.VMEM, pltpu.SMEM, pltpu.HBM

    src_scratch = [
        vmem((tgt_count, LANES), jnp.float32),
        vmem((rows + 1, 8, BLOCK), jnp.float32),
        vmem((rows + 1, 8, BLOCK), jnp.float32),
    ]
    tgt_scratch = [
        vmem((rows, BLOCK), jnp.float32),
        vmem((cols + 1, BLOCK, LANES), jnp.float32),
        vmem((cols + 1, BLOCK, LANES), jnp.float32),
    ]
    logs, src_held, src_sq, tgt_sq, reach, tall, pairs = call(
        first_src_kernel,
        [
            pltpu.with_memory_space_constraint(array, hbm)
            for array in (pattern.T, src_cells, tgt_cells, init_potential.reshape(tgt_shape))
        ],
        [hbm] * 4,
        [
            floats(*src_shape), jax.ShapeDtypeStruct(src_cells.shape, src_cells.dtype),
            floats(*src_shape), floats(*tgt_shape), floats(8, LANES),
            jax.ShapeDtypeStruct((tgt_count, depth), jnp.bfloat16),
            jax.ShapeDtypeStruct((rows * cols + GROUP + 1,), jnp.int32),
        ],
        [vmem] * 6 + [smem],
        [
            smem((cols, rows), jnp.int32), vmem(tgt_cells.shape, tgt_cells.dtype),
            vmem(tgt_shape, jnp.float32), pltpu.SemaphoreType.DMA((4,)),
        ] + src_scratch,
        "src_first",
    )
    for sweep in range(SWEEPS):
        if sweep:
            (logs,) = call(
                src_kernel, [pairs, src_held, tall, gathered, tgt_mass, reach], [smem] + [vmem] * 5,
                [floats(*src_shape)], [vmem], src_scratch, "src_next",
            )
        src_logs = over_tgt(logs)
        args = [pairs, src_held, tall, src_logs, src_mass, reach]
        if sweep < SWEEPS - 1:
            (logs,) = call(
                tgt_kernel, args, [smem] + [vmem] * 5, [floats(copies, *tgt_shape)], [vmem],
                tgt_scratch, "tgt",
            )
        else:
            logs, src_pot = call(
                last_tgt_kernel, args + [src_sq], [smem] + [vmem] * 6,
                [floats(copies, *tgt_shape), floats(*src_shape)], [vmem, hbm],
                tgt_scratch + [vmem(src_shape, jnp.float32), pltpu.SemaphoreType.DMA], "tgt_last",
            )
        gathered = lax.all_to_all(logs, "src", 0, 0)
    top = gathered.max(0)
    tgt_logs = top + jnp.log(jnp.exp(gathered - top[None]).sum(0))
    tgt_pot = tgt_sq + ENTROPY * (tgt_mass - tgt_logs)
    return src_pot.reshape(-1), tgt_pot.reshape(-1)


def solution(mesh):
    return jax.shard_map(
        local,
        mesh=mesh,
        in_specs=(P(None, "src"), P(None, "tgt"), P("src"), P("tgt"), P("tgt"), P("src", "tgt")),
        out_specs=(P("src"), P("tgt")),
        check_vma=False,
    )
```

```python
import jax
import jax.numpy as jnp
from jax import lax
from jax.experimental import pallas as pl
from jax.experimental.pallas import tpu as pltpu
from jax.sharding import PartitionSpec as P

BLOCK = 512
LANES = 128
PARTS = BLOCK // LANES
SWEEPS = 2
ENTROPY = 0.5
LOWEST = -1e30
CHUNKS = 4
GROUP = 8
HELD = 40
HELD_GROUP = 4
HELD_ROWS = 64
VMEM_LIMIT = 7 << 20
MERGE_LIMIT = 1 << 20


def list_pairs(pattern_ref, list_ref):
    cols, rows = pattern_ref.shape
    count = jnp.int32(0)
    for row in range(rows):
        for col in range(cols):
            list_ref[count] = row * cols + col
            count = count + pattern_ref[col, row]
    for extra in range(GROUP):
        list_ref[count + extra] = rows * cols
    list_ref[rows * cols + GROUP] = count


def blocks_of(ref):
    rows = ref.shape[0] // PARTS
    return jnp.concatenate([ref[pl.ds(part, rows, stride=PARTS), :] for part in range(PARTS)], axis=1)


def store_blocks(ref, values):
    rows = values.shape[0]
    for part in range(PARTS):
        ref[pl.ds(part, rows, stride=PARTS), :] = values[:, part * LANES : (part + 1) * LANES]


def factors(potential, reach):
    shift = jnp.max(potential, keepdims=True)
    extent = shift - jnp.min(potential, keepdims=True)
    fits = jnp.logical_and(reach <= 70.0, reach + extent <= 80.0)
    below = potential - shift
    safe = jnp.max(jnp.where(fits, 1.0, 0.0)) > 0.5
    return jnp.where(fits, jnp.exp(below), below), shift, safe


def log_or_lowest(total, top):
    some = total > 0.0
    return jnp.where(some, jnp.log(jnp.where(some, total, 1.0)) + top, LOWEST)


def run_pairs(list_ref, first, last, group, visit):
    def turn(width, base):
        def body(step, carry):
            for at in range(width):
                index = base + step * width + at
                visit(index, list_ref[index])
            return carry

        return body

    full = lax.div(last - first, group)
    middle = first + full * group
    lax.fori_loop(0, full, turn(group, first), 0)
    lax.fori_loop(0, lax.div(last - middle + 1, 2), turn(2, middle), 0)


def run_pairs_singly(list_ref, visit):
    def body(step, carry):
        visit(list_ref[step])
        return carry

    lax.fori_loop(0, count_of(list_ref), body, 0)


def count_of(list_ref):
    return list_ref[list_ref.shape[0] - 2]


def held_of(list_ref):
    return list_ref[list_ref.shape[0] - 1]


def place(pair, rows, cols):
    return lax.rem(lax.div(pair, cols), rows), lax.rem(pair, cols)


def tile_of(tall_ref, src_ref, src_block, tgt_block, start=0, size=BLOCK):
    left = tall_ref[pl.ds(pl.multiple_of(tgt_block * BLOCK + start, size), size), :]
    right = src_ref[:, pl.ds(pl.multiple_of(src_block * BLOCK, BLOCK), BLOCK)]
    return jnp.dot(left, right, preferred_element_type=jnp.float32)


def lane_part(values, part):
    return values[:, part * LANES : (part + 1) * LANES]


def fold_lanes(values, fold):
    out = lane_part(values, 0)
    for part in range(1, PARTS):
        out = fold(out, lane_part(values, part))
    return out


def spread_down(weights, spread_ref):
    for row in range(weights.shape[0]):
        down = jnp.broadcast_to(weights[row : row + 1, :], (LANES, LANES)).T
        spread_ref[row * LANES : (row + 1) * LANES, :] = down


def src_sums(
    potential, reach, fill, list_ref, held_ref, tall_ref, src_ref, spread_ref, sum_ref, top_ref, out_ref
):
    rows, cols = src_ref.shape[1] // BLOCK, tall_ref.shape[0] // BLOCK
    weights, shift, safe = factors(potential, reach)
    spread_down(weights, spread_ref)
    sum_ref[...] = jnp.zeros_like(sum_ref)
    count = count_of(list_ref)
    if fill:
        list_ref[list_ref.shape[0] - 1] = jnp.where(safe, jnp.minimum(count, HELD), 0)

    @pl.when(safe)
    def _():
        def visit(index, pair):
            src_block, tgt_block = place(pair, rows, cols)
            tile = jnp.exp(tile_of(tall_ref, src_ref, src_block, tgt_block))
            if fill:
                held_ref[jnp.minimum(index, HELD)] = tile
            down = spread_ref[pl.ds(pl.multiple_of(tgt_block * BLOCK, BLOCK), BLOCK), :]
            sums = [
                (lane_part(tile, part) * down).reshape(-1, 8, LANES).sum(0) for part in range(PARTS)
            ]
            sum_ref[lax.div(pair, cols)] += jnp.concatenate(sums, axis=1)

        def visit_held(index, pair):
            slot, base = jnp.minimum(index, HELD), lax.rem(pair, cols) * BLOCK
            sums = [jnp.zeros((8, LANES), jnp.float32)] * PARTS
            for start in range(0, BLOCK, HELD_ROWS):
                down = spread_ref[pl.ds(pl.multiple_of(base + start, HELD_ROWS), HELD_ROWS), :]
                for part in range(PARTS):
                    lanes = slice(part * LANES, (part + 1) * LANES)
                    tile = held_ref[slot, start : start + HELD_ROWS, lanes] * down
                    sums[part] = sums[part] + tile.reshape(-1, 8, LANES).sum(0)
            sum_ref[lax.div(pair, cols)] += jnp.concatenate(sums, axis=1)

        held = 0
        if not fill:
            held = held_of(list_ref)
            run_pairs(list_ref, 0, held, HELD_GROUP, visit_held)
        run_pairs(list_ref, held, count, GROUP, visit)
        store_blocks(out_ref, log_or_lowest(sum_ref[0:rows].sum(1), shift))

    @pl.when(jnp.logical_not(safe))
    def _():
        top_ref[...] = jnp.full_like(top_ref, LOWEST)

        def visit(pair):
            src_block, tgt_block = place(pair, rows, cols)

            def chunk(index, carry):
                start = pl.multiple_of(index * LANES, LANES)
                down = spread_ref[pl.ds(pl.multiple_of(tgt_block * BLOCK + start, LANES), LANES), :]
                tile = tile_of(tall_ref, src_ref, src_block, tgt_block, start, LANES)
                tile = (tile + jnp.concatenate([down] * PARTS, axis=1)).reshape(-1, 8, BLOCK)
                old = top_ref[src_block]
                new = jnp.maximum(old, tile.max(0))
                more = jnp.exp(tile - new[None]).sum(0)
                sum_ref[src_block] = sum_ref[src_block] * jnp.exp(old - new) + more
                top_ref[src_block] = new
                return carry

            lax.fori_loop(0, PARTS, chunk, 0)

        run_pairs_singly(list_ref, visit)
        slots = top_ref[0:rows]
        top = slots.max(1, keepdims=True)
        total = (sum_ref[0:rows] * jnp.exp(slots - top)).sum(1)
        store_blocks(out_ref, log_or_lowest(total, top[:, 0] + shift))


def tgt_sums(
    potential, reach, list_ref, held_ref, tall_ref, src_ref, weight_ref, sum_ref, top_ref, out_ref
):
    rows, cols = src_ref.shape[1] // BLOCK, tall_ref.shape[0] // BLOCK
    weights, shift, safe = factors(potential, reach)
    weight_ref[...] = weights
    sum_ref[...] = jnp.zeros_like(sum_ref)

    def store(block, total, top):
        values = log_or_lowest(total, top)
        for part in range(PARTS):
            at = block * PARTS + part
            out_ref[0, at : at + 1, :] = lane_part(values, part)

    @pl.when(safe)
    def _():
        def visit(index, pair):
            src_block, tgt_block = place(pair, rows, cols)
            at = jnp.where(pair < rows * cols, tgt_block, cols)
            tile = jnp.exp(tile_of(tall_ref, src_ref, src_block, tgt_block))
            sum_ref[at] += fold_lanes(tile * weight_ref[pl.ds(src_block, 1), :], jnp.add)

        def visit_held(index, pair):
            src_block, tgt_block = place(pair, rows, cols)
            at = jnp.where(pair < rows * cols, tgt_block, cols)
            slot = jnp.minimum(index, HELD)
            right = weight_ref[pl.ds(src_block, 1), :]
            for start in range(0, BLOCK, HELD_ROWS):
                tile = held_ref[slot, start : start + HELD_ROWS, :] * right
                sum_ref[at, start : start + HELD_ROWS, :] += fold_lanes(tile, jnp.add)

        held = held_of(list_ref)
        run_pairs(list_ref, 0, held, HELD_GROUP, visit_held)
        run_pairs(list_ref, held, count_of(list_ref), GROUP, visit)
        for block in range(cols):
            store(block, sum_ref[block].T.sum(0, keepdims=True), shift)

    @pl.when(jnp.logical_not(safe))
    def _():
        top_ref[...] = jnp.full_like(top_ref, LOWEST)

        def visit(pair):
            src_block, tgt_block = place(pair, rows, cols)
            right = weight_ref[pl.ds(src_block, 1), :]

            def chunk(index, carry):
                start = pl.multiple_of(index * LANES, LANES)
                tile = tile_of(tall_ref, src_ref, src_block, tgt_block, start, LANES) + right
                at = (tgt_block, pl.ds(start, LANES), slice(None))
                old = top_ref[at]
                new = jnp.maximum(old, fold_lanes(tile, jnp.maximum))
                more = fold_lanes(jnp.exp(tile - jnp.concatenate([new] * PARTS, axis=1)), jnp.add)
                sum_ref[at] = sum_ref[at] * jnp.exp(old - new) + more
                top_ref[at] = new
                return carry

            lax.fori_loop(0, PARTS, chunk, 0)

        run_pairs_singly(list_ref, visit)
        for block in range(cols):
            slots = top_ref[block].T
            top = slots.max(0, keepdims=True)
            total = (sum_ref[block].T * jnp.exp(slots - top)).sum(0, keepdims=True)
            store(block, total, top + shift)

    for copy in range(1, out_ref.shape[0]):
        out_ref[copy] = out_ref[0]


def store_squares(cells_ref, out_ref, first, count):
    for block in range(first, first + count):
        cells = cells_ref[:, block * BLOCK : (block + 1) * BLOCK].astype(jnp.float32)
        squares = jnp.sum(cells * cells, axis=0, keepdims=True)
        for part in range(PARTS):
            at = block * PARTS + part
            out_ref[at : at + 1, :] = lane_part(squares, part)


def first_src_kernel(
    pattern_hbm, src_hbm, tgt_hbm, pot_hbm, room_ref,
    out_ref, src_ref, src_sq_ref, tgt_sq_ref, reach_ref, tall_ref, list_ref, held_ref,
    pattern_ref, tgt_ref, pot_ref, sems, spread_ref, sum_ref, top_ref,
):
    tgt_copy, pattern_copy, pot_copy = copies = [
        pltpu.make_async_copy(source, target, sems.at[at])
        for at, (source, target) in enumerate(
            [(tgt_hbm, tgt_ref), (pattern_hbm, pattern_ref), (pot_hbm, pot_ref)]
        )
    ]
    width = src_ref.shape[1] // CHUNKS
    src_copies = []
    for chunk in range(CHUNKS):
        lanes = pl.ds(chunk * width, width)
        src_copies.append(
            pltpu.make_async_copy(src_hbm.at[:, lanes], src_ref.at[:, lanes], sems.at[3 + chunk])
        )
    for copy in copies + src_copies:
        copy.start()
    tgt_copy.wait()
    for block in range(tgt_ref.shape[1] // BLOCK):
        cells = tgt_ref[:, block * BLOCK : (block + 1) * BLOCK].astype(jnp.float32) * 4.0
        tall_ref[block * BLOCK : (block + 1) * BLOCK, :] = cells.T.astype(jnp.bfloat16)
    store_squares(tgt_ref, tgt_sq_ref, 0, tgt_ref.shape[1] // BLOCK)
    pattern_copy.wait()
    list_pairs(pattern_ref, list_ref)
    pot_copy.wait()
    for chunk in range(CHUNKS):
        src_copies[chunk].wait()
        store_squares(src_ref, src_sq_ref, chunk * width // BLOCK, width // BLOCK)
    reach = 4.0 * jnp.sqrt(jnp.max(src_sq_ref[...], keepdims=True)) * jnp.sqrt(
        jnp.max(tgt_sq_ref[...], keepdims=True)
    )
    reach_ref[...] = jnp.broadcast_to(reach, reach_ref.shape)
    potential = 2.0 * (pot_ref[...] - tgt_sq_ref[...])
    src_sums(
        potential, reach, True, list_ref, held_ref, tall_ref, src_ref, spread_ref, sum_ref,
        top_ref, out_ref,
    )


def src_kernel(
    list_ref, held_ref, src_ref, tall_ref, gathered_ref, mass_ref, reach_ref,
    out_ref,
    spread_ref, sum_ref, top_ref,
):
    gathered = gathered_ref[...]
    top = gathered.max(0)
    potential = mass_ref[...] - (top + jnp.log(jnp.exp(gathered - top[None]).sum(0)))
    src_sums(
        potential, reach_ref[0:1, 0:1], False, list_ref, held_ref, tall_ref, src_ref, spread_ref,
        sum_ref, top_ref, out_ref,
    )


def tgt_kernel(
    list_ref, held_ref, src_ref, tall_ref, logs_ref, mass_ref, reach_ref,
    out_ref,
    weight_ref, sum_ref, top_ref,
):
    potential = blocks_of(mass_ref) - blocks_of(logs_ref)
    tgt_sums(
        potential, reach_ref[0:1, 0:1], list_ref, held_ref, tall_ref, src_ref, weight_ref, sum_ref,
        top_ref, out_ref,
    )


def last_tgt_kernel(
    list_ref, held_ref, src_ref, tall_ref, logs_ref, mass_ref, reach_ref, src_sq_ref,
    out_ref, src_pot_hbm,
    weight_ref, sum_ref, top_ref, src_pot_ref, sem,
):
    src_pot_ref[...] = src_sq_ref[...] + ENTROPY * (mass_ref[...] - logs_ref[...])
    copy = pltpu.make_async_copy(src_pot_ref, src_pot_hbm, sem)
    copy.start()
    tgt_kernel(
        list_ref, held_ref, src_ref, tall_ref, logs_ref, mass_ref, reach_ref, out_ref, weight_ref,
        sum_ref, top_ref,
    )
    copy.wait()


def call(kernel, args, in_spaces, outs, out_spaces, scratch, name, limit=VMEM_LIMIT, aliases={}):
    return pl.pallas_call(
        kernel,
        out_shape=outs,
        in_specs=[pl.BlockSpec(memory_space=space) for space in in_spaces],
        out_specs=[pl.BlockSpec(memory_space=space) for space in out_spaces],
        scratch_shapes=scratch,
        compiler_params=pltpu.CompilerParams(vmem_limit_bytes=limit),
        name=name,
        input_output_aliases=aliases,
    )(*args)


def floats(*shape):
    return jax.ShapeDtypeStruct(shape, jnp.float32)


def merge_two_kernel(one_ref, other_ref, out_ref):
    one, other = one_ref[...], other_ref[...]
    out_ref[...] = jnp.maximum(one, other) + jnp.log(1.0 + jnp.exp(-jnp.abs(one - other)))


def merge_kernel(own_ref, one_ref, two_ref, three_ref, out_ref):
    own, one, two, three = own_ref[...], one_ref[...], two_ref[...], three_ref[...]
    top = jnp.maximum(jnp.maximum(own, one), jnp.maximum(two, three))
    near = jnp.exp(own - top) + jnp.exp(one - top)
    far = jnp.exp(two - top) + jnp.exp(three - top)
    out_ref[...] = top + jnp.log(near + far)


def over_tgt(logs):
    size = lax.axis_size("tgt")

    def from_peer(values, mask):
        return lax.ppermute(values, "tgt", [(at, at ^ mask) for at in range(size)])

    (logs,) = call(
        merge_two_kernel, [logs, from_peer(logs, 1)], [pltpu.VMEM] * 2, [floats(*logs.shape)],
        [pltpu.VMEM], [], "merge_two", MERGE_LIMIT,
    )
    for stage in (2, 8):
        peers = [from_peer(logs, stage * mask) for mask in (1, 2, 3)]
        (logs,) = call(
            merge_kernel, [logs] + peers, [pltpu.VMEM] * 4, [floats(*logs.shape)], [pltpu.VMEM], [],
            "merge", MERGE_LIMIT,
        )
    return logs


def local(src_cells, tgt_cells, src_logmass, tgt_logmass, init_potential, pattern):
    copies = lax.axis_size("src")
    depth, src_count = src_cells.shape
    tgt_count = tgt_cells.shape[1]
    rows, cols = pattern.shape
    src_shape = (src_count // LANES, LANES)
    tgt_shape = (tgt_count // LANES, LANES)
    src_mass = src_logmass.reshape(src_shape)
    tgt_mass = tgt_logmass.reshape(tgt_shape)
    vmem, smem, hbm = pltpu.VMEM, pltpu.SMEM, pltpu.HBM

    src_scratch = [
        vmem((tgt_count, LANES), jnp.float32),
        vmem((rows + 1, 8, BLOCK), jnp.float32),
        vmem((rows + 1, 8, BLOCK), jnp.float32),
    ]
    tgt_scratch = [
        vmem((rows, BLOCK), jnp.float32),
        vmem((cols + 1, BLOCK, LANES), jnp.float32),
        vmem((cols + 1, BLOCK, LANES), jnp.float32),
    ]
    (room,) = call(
        lambda room_ref: None, [], [], [vmem((HELD + 1, BLOCK, BLOCK), jnp.float32)], [vmem], [], "room",
        MERGE_LIMIT,
    )
    logs, src_kept, src_sq, tgt_sq, reach, tall, pairs, held = call(
        first_src_kernel,
        [
            pltpu.with_memory_space_constraint(array, hbm)
            for array in (pattern.T, src_cells, tgt_cells, init_potential.reshape(tgt_shape))
        ]
        + [pltpu.with_memory_space_constraint(room, vmem)],
        [hbm] * 4 + [vmem],
        [
            floats(*src_shape), jax.ShapeDtypeStruct(src_cells.shape, src_cells.dtype),
            floats(*src_shape), floats(*tgt_shape), floats(8, LANES),
            jax.ShapeDtypeStruct((tgt_count, depth), jnp.bfloat16),
            jax.ShapeDtypeStruct((rows * cols + GROUP + 2,), jnp.int32),
            vmem((HELD + 1, BLOCK, BLOCK), jnp.float32),
        ],
        [vmem] * 6 + [smem, vmem],
        [
            smem((cols, rows), jnp.int32), vmem(tgt_cells.shape, tgt_cells.dtype),
            vmem(tgt_shape, jnp.float32), pltpu.SemaphoreType.DMA((3 + CHUNKS,)),
        ] + src_scratch,
        "src_first", aliases={4: 7},
    )
    held = pltpu.with_memory_space_constraint(held, vmem)
    for sweep in range(SWEEPS):
        if sweep:
            (logs,) = call(
                src_kernel, [pairs, held, src_kept, tall, gathered, tgt_mass, reach], [smem] + [vmem] * 6,
                [floats(*src_shape)], [vmem], src_scratch, "src_next",
            )
        logs = over_tgt(logs)
        args = [pairs, held, src_kept, tall, logs, src_mass, reach]
        if sweep < SWEEPS - 1:
            (logs,) = call(
                tgt_kernel, args, [smem] + [vmem] * 6, [floats(copies, *tgt_shape)], [vmem],
                tgt_scratch, "tgt",
            )
        else:
            logs, src_pot = call(
                last_tgt_kernel, args + [src_sq], [smem] + [vmem] * 7,
                [floats(copies, *tgt_shape), floats(*src_shape)], [vmem, hbm],
                tgt_scratch + [vmem(src_shape, jnp.float32), pltpu.SemaphoreType.DMA], "tgt_last",
            )
        gathered = lax.all_to_all(logs, "src", 0, 0)
    top = gathered.max(0)
    tgt_logs = top + jnp.log(jnp.exp(gathered - top[None]).sum(0))
    tgt_pot = tgt_sq + ENTROPY * (tgt_mass - tgt_logs)
    return src_pot.reshape(-1), tgt_pot.reshape(-1)


def solution(mesh):
    return jax.shard_map(
        local,
        mesh=mesh,
        in_specs=(P(None, "src"), P(None, "tgt"), P("src"), P("tgt"), P("tgt"), P("src", "tgt")),
        out_specs=(P("src"), P("tgt")),
        check_vma=False,
    )
```

```python
import jax
import jax.numpy as jnp
from jax import lax
from jax.experimental import pallas as pl
from jax.experimental.pallas import tpu as pltpu
from jax.sharding import PartitionSpec as P

BLOCK = 512
LANES = 128
PARTS = BLOCK // LANES
SWEEPS = 2
ENTROPY = 0.5
LOWEST = -1e30
CHUNKS = 4
GROUP = 8
HELD = 42
HELD_GROUP = 6
HELD_ROWS = 64
VMEM_LIMIT = 7 << 20
MERGE_LIMIT = 1 << 20


def list_pairs(pattern_ref, list_ref):
    cols, rows = pattern_ref.shape
    count = jnp.int32(0)
    for row in range(rows):
        for col in range(cols):
            list_ref[count] = row * cols + col
            count = count + pattern_ref[col, row]
    for extra in range(GROUP):
        list_ref[count + extra] = rows * cols
    list_ref[rows * cols + GROUP] = count


def blocks_of(ref):
    rows = ref.shape[0] // PARTS
    return jnp.concatenate([ref[pl.ds(part, rows, stride=PARTS), :] for part in range(PARTS)], axis=1)


def store_blocks(ref, values):
    rows = values.shape[0]
    for part in range(PARTS):
        ref[pl.ds(part, rows, stride=PARTS), :] = values[:, part * LANES : (part + 1) * LANES]


def factors(potential, reach):
    shift = jnp.max(potential, keepdims=True)
    extent = shift - jnp.min(potential, keepdims=True)
    fits = jnp.logical_and(reach <= 70.0, reach + extent <= 80.0)
    below = potential - shift
    safe = jnp.max(jnp.where(fits, 1.0, 0.0)) > 0.5
    return jnp.where(fits, jnp.exp(below), below), shift, safe


def log_or_lowest(total, top):
    some = total > 0.0
    return jnp.where(some, jnp.log(jnp.where(some, total, 1.0)) + top, LOWEST)


def run_pairs(list_ref, first, last, group, visit):
    def turn(width, base):
        def body(step, carry):
            for at in range(width):
                index = base + step * width + at
                visit(index, list_ref[index])
            return carry

        return body

    full = lax.div(last - first, group)
    middle = first + full * group
    lax.fori_loop(0, full, turn(group, first), 0)
    lax.fori_loop(0, lax.div(last - middle + 1, 2), turn(2, middle), 0)


def run_pairs_singly(list_ref, visit):
    def body(step, carry):
        visit(list_ref[step])
        return carry

    lax.fori_loop(0, count_of(list_ref), body, 0)


def count_of(list_ref):
    return list_ref[list_ref.shape[0] - 2]


def held_of(list_ref):
    return list_ref[list_ref.shape[0] - 1]


def place(pair, rows, cols):
    return lax.rem(lax.div(pair, cols), rows), lax.rem(pair, cols)


def tile_of(tall_ref, src_ref, src_block, tgt_block, start=0, size=BLOCK):
    left = tall_ref[pl.ds(pl.multiple_of(tgt_block * BLOCK + start, size), size), :]
    right = src_ref[:, pl.ds(pl.multiple_of(src_block * BLOCK, BLOCK), BLOCK)]
    return jnp.dot(left, right, preferred_element_type=jnp.float32)


def lane_part(values, part):
    return values[:, part * LANES : (part + 1) * LANES]


def fold_lanes(values, fold):
    out = lane_part(values, 0)
    for part in range(1, PARTS):
        out = fold(out, lane_part(values, part))
    return out


def spread_down(weights, spread_ref):
    for row in range(weights.shape[0]):
        down = jnp.broadcast_to(weights[row : row + 1, :], (LANES, LANES)).T
        spread_ref[row * LANES : (row + 1) * LANES, :] = down


def src_sums(
    potential, reach, fill, list_ref, held_ref, tall_ref, src_ref, spread_ref, sum_ref, top_ref, out_ref
):
    rows, cols = src_ref.shape[1] // BLOCK, tall_ref.shape[0] // BLOCK
    weights, shift, safe = factors(potential, reach)
    spread_down(weights, spread_ref)
    sum_ref[...] = jnp.zeros_like(sum_ref)
    count = count_of(list_ref)
    if fill:
        list_ref[list_ref.shape[0] - 1] = jnp.where(safe, jnp.minimum(count, HELD), 0)

    @pl.when(safe)
    def _():
        def visit(index, pair):
            src_block, tgt_block = place(pair, rows, cols)
            tile = jnp.exp(tile_of(tall_ref, src_ref, src_block, tgt_block))
            if fill:
                held_ref[jnp.minimum(index, HELD)] = tile
            down = spread_ref[pl.ds(pl.multiple_of(tgt_block * BLOCK, BLOCK), BLOCK), :]
            sums = [
                (lane_part(tile, part) * down).reshape(-1, 8, LANES).sum(0) for part in range(PARTS)
            ]
            sum_ref[lax.div(pair, cols)] += jnp.concatenate(sums, axis=1)

        def visit_held(index, pair):
            slot, base = jnp.minimum(index, HELD), lax.rem(pair, cols) * BLOCK
            sums = [jnp.zeros((8, LANES), jnp.float32)] * PARTS
            for start in range(0, BLOCK, HELD_ROWS):
                down = spread_ref[pl.ds(pl.multiple_of(base + start, HELD_ROWS), HELD_ROWS), :]
                for part in range(PARTS):
                    lanes = slice(part * LANES, (part + 1) * LANES)
                    tile = held_ref[slot, start : start + HELD_ROWS, lanes] * down
                    sums[part] = sums[part] + tile.reshape(-1, 8, LANES).sum(0)
            sum_ref[lax.div(pair, cols)] += jnp.concatenate(sums, axis=1)

        held = 0
        if not fill:
            held = held_of(list_ref)
            run_pairs(list_ref, 0, held, HELD_GROUP, visit_held)
        run_pairs(list_ref, held, count, GROUP, visit)
        store_blocks(out_ref, log_or_lowest(sum_ref[0:rows].sum(1), shift))

    @pl.when(jnp.logical_not(safe))
    def _():
        top_ref[...] = jnp.full_like(top_ref, LOWEST)

        def visit(pair):
            src_block, tgt_block = place(pair, rows, cols)

            def chunk(index, carry):
                start = pl.multiple_of(index * LANES, LANES)
                down = spread_ref[pl.ds(pl.multiple_of(tgt_block * BLOCK + start, LANES), LANES), :]
                tile = tile_of(tall_ref, src_ref, src_block, tgt_block, start, LANES)
                tile = (tile + jnp.concatenate([down] * PARTS, axis=1)).reshape(-1, 8, BLOCK)
                old = top_ref[src_block]
                new = jnp.maximum(old, tile.max(0))
                more = jnp.exp(tile - new[None]).sum(0)
                sum_ref[src_block] = sum_ref[src_block] * jnp.exp(old - new) + more
                top_ref[src_block] = new
                return carry

            lax.fori_loop(0, PARTS, chunk, 0)

        run_pairs_singly(list_ref, visit)
        slots = top_ref[0:rows]
        top = slots.max(1, keepdims=True)
        total = (sum_ref[0:rows] * jnp.exp(slots - top)).sum(1)
        store_blocks(out_ref, log_or_lowest(total, top[:, 0] + shift))


def tgt_sums(
    potential, reach, list_ref, held_ref, tall_ref, src_ref, weight_ref, sum_ref, top_ref, out_ref
):
    rows, cols = src_ref.shape[1] // BLOCK, tall_ref.shape[0] // BLOCK
    weights, shift, safe = factors(potential, reach)
    weight_ref[...] = weights
    sum_ref[...] = jnp.zeros_like(sum_ref)

    def store(block, total, top):
        values = log_or_lowest(total, top)
        for part in range(PARTS):
            at = block * PARTS + part
            out_ref[0, at : at + 1, :] = lane_part(values, part)

    @pl.when(safe)
    def _():
        def visit(index, pair):
            src_block, tgt_block = place(pair, rows, cols)
            at = jnp.where(pair < rows * cols, tgt_block, cols)
            tile = jnp.exp(tile_of(tall_ref, src_ref, src_block, tgt_block))
            sum_ref[at] += fold_lanes(tile * weight_ref[pl.ds(src_block, 1), :], jnp.add)

        def visit_held(index, pair):
            src_block, tgt_block = place(pair, rows, cols)
            at = jnp.where(pair < rows * cols, tgt_block, cols)
            slot = jnp.minimum(index, HELD)
            right = weight_ref[pl.ds(src_block, 1), :]
            for start in range(0, BLOCK, HELD_ROWS):
                tile = held_ref[slot, start : start + HELD_ROWS, :] * right
                sum_ref[at, start : start + HELD_ROWS, :] += fold_lanes(tile, jnp.add)

        held = held_of(list_ref)
        run_pairs(list_ref, 0, held, HELD_GROUP, visit_held)
        run_pairs(list_ref, held, count_of(list_ref), GROUP, visit)
        for block in range(cols):
            store(block, sum_ref[block].T.sum(0, keepdims=True), shift)

    @pl.when(jnp.logical_not(safe))
    def _():
        top_ref[...] = jnp.full_like(top_ref, LOWEST)

        def visit(pair):
            src_block, tgt_block = place(pair, rows, cols)
            right = weight_ref[pl.ds(src_block, 1), :]

            def chunk(index, carry):
                start = pl.multiple_of(index * LANES, LANES)
                tile = tile_of(tall_ref, src_ref, src_block, tgt_block, start, LANES) + right
                at = (tgt_block, pl.ds(start, LANES), slice(None))
                old = top_ref[at]
                new = jnp.maximum(old, fold_lanes(tile, jnp.maximum))
                more = fold_lanes(jnp.exp(tile - jnp.concatenate([new] * PARTS, axis=1)), jnp.add)
                sum_ref[at] = sum_ref[at] * jnp.exp(old - new) + more
                top_ref[at] = new
                return carry

            lax.fori_loop(0, PARTS, chunk, 0)

        run_pairs_singly(list_ref, visit)
        for block in range(cols):
            slots = top_ref[block].T
            top = slots.max(0, keepdims=True)
            total = (sum_ref[block].T * jnp.exp(slots - top)).sum(0, keepdims=True)
            store(block, total, top + shift)

    for copy in range(1, out_ref.shape[0]):
        out_ref[copy] = out_ref[0]


def store_squares(cells_ref, out_ref, first, count):
    for block in range(first, first + count):
        cells = cells_ref[:, block * BLOCK : (block + 1) * BLOCK].astype(jnp.float32)
        squares = jnp.sum(cells * cells, axis=0, keepdims=True)
        for part in range(PARTS):
            at = block * PARTS + part
            out_ref[at : at + 1, :] = lane_part(squares, part)


def first_src_kernel(
    pattern_hbm, src_hbm, tgt_hbm, pot_hbm, room_ref,
    out_ref, src_ref, src_sq_ref, tgt_sq_ref, reach_ref, tall_ref, list_ref, held_ref,
    pattern_ref, tgt_ref, pot_ref, sems, spread_ref, sum_ref, top_ref,
):
    tgt_copy, pattern_copy, pot_copy = copies = [
        pltpu.make_async_copy(source, target, sems.at[at])
        for at, (source, target) in enumerate(
            [(tgt_hbm, tgt_ref), (pattern_hbm, pattern_ref), (pot_hbm, pot_ref)]
        )
    ]
    width = src_ref.shape[1] // CHUNKS
    src_copies = []
    for chunk in range(CHUNKS):
        lanes = pl.ds(chunk * width, width)
        src_copies.append(
            pltpu.make_async_copy(src_hbm.at[:, lanes], src_ref.at[:, lanes], sems.at[3 + chunk])
        )
    for copy in copies + src_copies:
        copy.start()
    tgt_copy.wait()
    pattern_copy.wait()
    list_pairs(pattern_ref, list_ref)
    for block in range(tgt_ref.shape[1] // BLOCK):
        cells = tgt_ref[:, block * BLOCK : (block + 1) * BLOCK].astype(jnp.float32) * 4.0
        tall_ref[block * BLOCK : (block + 1) * BLOCK, :] = cells.T.astype(jnp.bfloat16)
    store_squares(tgt_ref, tgt_sq_ref, 0, tgt_ref.shape[1] // BLOCK)
    pot_copy.wait()
    for copy in src_copies:
        copy.wait()
    store_squares(src_ref, src_sq_ref, 0, src_ref.shape[1] // BLOCK)
    reach = 4.0 * jnp.sqrt(jnp.max(src_sq_ref[...], keepdims=True)) * jnp.sqrt(
        jnp.max(tgt_sq_ref[...], keepdims=True)
    )
    reach_ref[...] = jnp.broadcast_to(reach, reach_ref.shape)
    potential = 2.0 * (pot_ref[...] - tgt_sq_ref[...])
    src_sums(
        potential, reach, True, list_ref, held_ref, tall_ref, src_ref, spread_ref, sum_ref,
        top_ref, out_ref,
    )


def src_kernel(
    list_ref, held_ref, src_ref, tall_ref, gathered_ref, mass_ref, reach_ref,
    out_ref,
    spread_ref, sum_ref, top_ref,
):
    gathered = gathered_ref[...]
    top = gathered.max(0)
    potential = mass_ref[...] - (top + jnp.log(jnp.exp(gathered - top[None]).sum(0)))
    src_sums(
        potential, reach_ref[0:1, 0:1], False, list_ref, held_ref, tall_ref, src_ref, spread_ref,
        sum_ref, top_ref, out_ref,
    )


def tgt_kernel(
    list_ref, held_ref, src_ref, tall_ref, logs_ref, mass_ref, reach_ref,
    out_ref,
    weight_ref, sum_ref, top_ref,
):
    potential = blocks_of(mass_ref) - blocks_of(logs_ref)
    tgt_sums(
        potential, reach_ref[0:1, 0:1], list_ref, held_ref, tall_ref, src_ref, weight_ref, sum_ref,
        top_ref, out_ref,
    )


def last_tgt_kernel(
    list_ref, held_ref, src_ref, tall_ref, logs_ref, mass_ref, reach_ref, src_sq_ref,
    out_ref, src_pot_hbm,
    weight_ref, sum_ref, top_ref, src_pot_ref, sem,
):
    src_pot_ref[...] = src_sq_ref[...] + ENTROPY * (mass_ref[...] - logs_ref[...])
    copy = pltpu.make_async_copy(src_pot_ref, src_pot_hbm, sem)
    copy.start()
    tgt_kernel(
        list_ref, held_ref, src_ref, tall_ref, logs_ref, mass_ref, reach_ref, out_ref, weight_ref,
        sum_ref, top_ref,
    )
    copy.wait()


def call(kernel, args, in_spaces, outs, out_spaces, scratch, name, limit=VMEM_LIMIT, aliases={}):
    return pl.pallas_call(
        kernel,
        out_shape=outs,
        in_specs=[pl.BlockSpec(memory_space=space) for space in in_spaces],
        out_specs=[pl.BlockSpec(memory_space=space) for space in out_spaces],
        scratch_shapes=scratch,
        compiler_params=pltpu.CompilerParams(vmem_limit_bytes=limit),
        name=name,
        input_output_aliases=aliases,
    )(*args)


def floats(*shape):
    return jax.ShapeDtypeStruct(shape, jnp.float32)


def merge_two_kernel(one_ref, other_ref, out_ref):
    one, other = one_ref[...], other_ref[...]
    out_ref[...] = jnp.maximum(one, other) + jnp.log(1.0 + jnp.exp(-jnp.abs(one - other)))


def merge_kernel(own_ref, one_ref, two_ref, three_ref, out_ref):
    own, one, two, three = own_ref[...], one_ref[...], two_ref[...], three_ref[...]
    top = jnp.maximum(jnp.maximum(own, one), jnp.maximum(two, three))
    near = jnp.exp(own - top) + jnp.exp(one - top)
    far = jnp.exp(two - top) + jnp.exp(three - top)
    out_ref[...] = top + jnp.log(near + far)


def over_tgt(logs):
    size = lax.axis_size("tgt")

    def from_peer(values, mask):
        return lax.ppermute(values, "tgt", [(at, at ^ mask) for at in range(size)])

    (logs,) = call(
        merge_two_kernel, [logs, from_peer(logs, 1)], [pltpu.VMEM] * 2, [floats(*logs.shape)],
        [pltpu.VMEM], [], "merge_two", MERGE_LIMIT,
    )
    for stage in (2, 8):
        peers = [from_peer(logs, stage * mask) for mask in (1, 2, 3)]
        (logs,) = call(
            merge_kernel, [logs] + peers, [pltpu.VMEM] * 4, [floats(*logs.shape)], [pltpu.VMEM], [],
            "merge", MERGE_LIMIT,
        )
    return logs


def local(src_cells, tgt_cells, src_logmass, tgt_logmass, init_potential, pattern):
    copies = lax.axis_size("src")
    depth, src_count = src_cells.shape
    tgt_count = tgt_cells.shape[1]
    rows, cols = pattern.shape
    src_shape = (src_count // LANES, LANES)
    tgt_shape = (tgt_count // LANES, LANES)
    src_mass = src_logmass.reshape(src_shape)
    tgt_mass = tgt_logmass.reshape(tgt_shape)
    vmem, smem, hbm = pltpu.VMEM, pltpu.SMEM, pltpu.HBM

    src_scratch = [
        vmem((tgt_count, LANES), jnp.float32),
        vmem((rows + 1, 8, BLOCK), jnp.float32),
        vmem((rows + 1, 8, BLOCK), jnp.float32),
    ]
    tgt_scratch = [
        vmem((rows, BLOCK), jnp.float32),
        vmem((cols + 1, BLOCK, LANES), jnp.float32),
        vmem((cols + 1, BLOCK, LANES), jnp.float32),
    ]
    (room,) = call(
        lambda room_ref: None, [], [], [vmem((HELD + 1, BLOCK, BLOCK), jnp.float32)], [vmem], [], "room",
        MERGE_LIMIT,
    )
    logs, src_kept, src_sq, tgt_sq, reach, tall, pairs, held = call(
        first_src_kernel,
        [
            pltpu.with_memory_space_constraint(array, hbm)
            for array in (pattern.T, src_cells, tgt_cells, init_potential.reshape(tgt_shape))
        ]
        + [pltpu.with_memory_space_constraint(room, vmem)],
        [hbm] * 4 + [vmem],
        [
            floats(*src_shape), jax.ShapeDtypeStruct(src_cells.shape, src_cells.dtype),
            floats(*src_shape), floats(*tgt_shape), floats(8, LANES),
            jax.ShapeDtypeStruct((tgt_count, depth), jnp.bfloat16),
            jax.ShapeDtypeStruct((rows * cols + GROUP + 2,), jnp.int32),
            vmem((HELD + 1, BLOCK, BLOCK), jnp.float32),
        ],
        [vmem] * 6 + [smem, vmem],
        [
            smem((cols, rows), jnp.int32), vmem(tgt_cells.shape, tgt_cells.dtype),
            vmem(tgt_shape, jnp.float32), pltpu.SemaphoreType.DMA((3 + CHUNKS,)),
        ] + src_scratch,
        "src_first", aliases={4: 7},
    )
    held = pltpu.with_memory_space_constraint(held, vmem)
    for sweep in range(SWEEPS):
        if sweep:
            (logs,) = call(
                src_kernel, [pairs, held, src_kept, tall, gathered, tgt_mass, reach], [smem] + [vmem] * 6,
                [floats(*src_shape)], [vmem], src_scratch, "src_next",
            )
        logs = over_tgt(logs)
        args = [pairs, held, src_kept, tall, logs, src_mass, reach]
        if sweep < SWEEPS - 1:
            (logs,) = call(
                tgt_kernel, args, [smem] + [vmem] * 6, [floats(copies, *tgt_shape)], [vmem],
                tgt_scratch, "tgt",
            )
        else:
            logs, src_pot = call(
                last_tgt_kernel, args + [src_sq], [smem] + [vmem] * 7,
                [floats(copies, *tgt_shape), floats(*src_shape)], [vmem, hbm],
                tgt_scratch + [vmem(src_shape, jnp.float32), pltpu.SemaphoreType.DMA], "tgt_last",
            )
        gathered = lax.all_to_all(logs, "src", 0, 0)
    top = gathered.max(0)
    tgt_logs = top + jnp.log(jnp.exp(gathered - top[None]).sum(0))
    tgt_pot = tgt_sq + ENTROPY * (tgt_mass - tgt_logs)
    return src_pot.reshape(-1), tgt_pot.reshape(-1)


def solution(mesh):
    return jax.shard_map(
        local,
        mesh=mesh,
        in_specs=(P(None, "src"), P(None, "tgt"), P("src"), P("tgt"), P("tgt"), P("src", "tgt")),
        out_specs=(P("src"), P("tgt")),
        check_vma=False,
    )
```

```python
import jax
import jax.numpy as jnp
from jax import lax
from jax.experimental import pallas as pl
from jax.experimental.pallas import tpu as pltpu
from jax.sharding import PartitionSpec as P

BLOCK = 512
LANES = 128
PARTS = BLOCK // LANES
SWEEPS = 2
ENTROPY = 0.5
LOWEST = -1e30
CHUNKS = 4
GROUP = 16
HELD = 42
HELD_GROUP = 6
HELD_ROWS = 64
VMEM_LIMIT = 7 << 20
MERGE_LIMIT = 1 << 20


def list_pairs(pattern_ref, list_ref):
    cols, rows = pattern_ref.shape
    count = jnp.int32(0)
    for row in range(rows):
        for col in range(cols):
            list_ref[count] = row * cols + col
            count = count + pattern_ref[col, row]
    for extra in range(GROUP):
        list_ref[count + extra] = rows * cols
    list_ref[rows * cols + GROUP] = count


def blocks_of(ref):
    rows = ref.shape[0] // PARTS
    return jnp.concatenate([ref[pl.ds(part, rows, stride=PARTS), :] for part in range(PARTS)], axis=1)


def store_blocks(ref, values):
    rows = values.shape[0]
    for part in range(PARTS):
        ref[pl.ds(part, rows, stride=PARTS), :] = values[:, part * LANES : (part + 1) * LANES]


def factors(potential, reach):
    shift = jnp.max(potential, keepdims=True)
    extent = shift - jnp.min(potential, keepdims=True)
    fits = jnp.logical_and(reach <= 70.0, reach + extent <= 80.0)
    below = potential - shift
    safe = jnp.max(jnp.where(fits, 1.0, 0.0)) > 0.5
    return jnp.where(fits, jnp.exp(below), below), shift, safe


def log_or_lowest(total, top):
    some = total > 0.0
    return jnp.where(some, jnp.log(jnp.where(some, total, 1.0)) + top, LOWEST)


def run_pairs(list_ref, first, last, group, visit):
    def turn(width, base):
        def body(step, carry):
            for at in range(width):
                index = base + step * width + at
                visit(index, list_ref[index])
            return carry

        return body

    at = first
    for width in (group, group // 2):
        full = lax.div(last - at, width)
        lax.fori_loop(0, full, turn(width, at), 0)
        at = at + full * width
    lax.fori_loop(0, lax.div(last - at + 1, 2), turn(2, at), 0)


def run_pairs_singly(list_ref, visit):
    def body(step, carry):
        visit(list_ref[step])
        return carry

    lax.fori_loop(0, count_of(list_ref), body, 0)


def count_of(list_ref):
    return list_ref[list_ref.shape[0] - 2]


def held_of(list_ref):
    return list_ref[list_ref.shape[0] - 1]


def place(pair, rows, cols):
    return lax.rem(lax.div(pair, cols), rows), lax.rem(pair, cols)


def tile_of(tall_ref, src_ref, src_block, tgt_block, start=0, size=BLOCK):
    left = tall_ref[pl.ds(pl.multiple_of(tgt_block * BLOCK + start, size), size), :]
    right = src_ref[:, pl.ds(pl.multiple_of(src_block * BLOCK, BLOCK), BLOCK)]
    return jnp.dot(left, right, preferred_element_type=jnp.float32)


def lane_part(values, part):
    return values[:, part * LANES : (part + 1) * LANES]


def fold_lanes(values, fold):
    out = lane_part(values, 0)
    for part in range(1, PARTS):
        out = fold(out, lane_part(values, part))
    return out


def spread_down(weights, spread_ref):
    for row in range(weights.shape[0]):
        down = jnp.broadcast_to(weights[row : row + 1, :], (LANES, LANES)).T
        spread_ref[row * LANES : (row + 1) * LANES, :] = down


def src_sums(
    potential, reach, fill, list_ref, held_ref, tall_ref, src_ref, spread_ref, sum_ref, top_ref, out_ref
):
    rows, cols = src_ref.shape[1] // BLOCK, tall_ref.shape[0] // BLOCK
    weights, shift, safe = factors(potential, reach)
    spread_down(weights, spread_ref)
    sum_ref[...] = jnp.zeros_like(sum_ref)
    count = count_of(list_ref)
    if fill:
        list_ref[list_ref.shape[0] - 1] = jnp.where(safe, jnp.minimum(count, HELD), 0)

    @pl.when(safe)
    def _():
        def visit(index, pair):
            src_block, tgt_block = place(pair, rows, cols)
            tile = jnp.exp(tile_of(tall_ref, src_ref, src_block, tgt_block))
            if fill:
                held_ref[jnp.minimum(index, HELD)] = tile
            down = spread_ref[pl.ds(pl.multiple_of(tgt_block * BLOCK, BLOCK), BLOCK), :]
            sums = [
                (lane_part(tile, part) * down).reshape(-1, 8, LANES).sum(0) for part in range(PARTS)
            ]
            sum_ref[lax.div(pair, cols)] += jnp.concatenate(sums, axis=1)

        def visit_held(index, pair):
            slot, base = jnp.minimum(index, HELD), lax.rem(pair, cols) * BLOCK
            sums = [jnp.zeros((8, LANES), jnp.float32)] * PARTS
            for start in range(0, BLOCK, HELD_ROWS):
                down = spread_ref[pl.ds(pl.multiple_of(base + start, HELD_ROWS), HELD_ROWS), :]
                for part in range(PARTS):
                    lanes = slice(part * LANES, (part + 1) * LANES)
                    tile = held_ref[slot, start : start + HELD_ROWS, lanes] * down
                    sums[part] = sums[part] + tile.reshape(-1, 8, LANES).sum(0)
            sum_ref[lax.div(pair, cols)] += jnp.concatenate(sums, axis=1)

        held = 0
        if not fill:
            held = held_of(list_ref)
            run_pairs(list_ref, 0, held, HELD_GROUP, visit_held)
        run_pairs(list_ref, held, count, GROUP, visit)
        store_blocks(out_ref, log_or_lowest(sum_ref[0:rows].sum(1), shift))

    @pl.when(jnp.logical_not(safe))
    def _():
        top_ref[...] = jnp.full_like(top_ref, LOWEST)

        def visit(pair):
            src_block, tgt_block = place(pair, rows, cols)

            def chunk(index, carry):
                start = pl.multiple_of(index * LANES, LANES)
                down = spread_ref[pl.ds(pl.multiple_of(tgt_block * BLOCK + start, LANES), LANES), :]
                tile = tile_of(tall_ref, src_ref, src_block, tgt_block, start, LANES)
                tile = (tile + jnp.concatenate([down] * PARTS, axis=1)).reshape(-1, 8, BLOCK)
                old = top_ref[src_block]
                new = jnp.maximum(old, tile.max(0))
                more = jnp.exp(tile - new[None]).sum(0)
                sum_ref[src_block] = sum_ref[src_block] * jnp.exp(old - new) + more
                top_ref[src_block] = new
                return carry

            lax.fori_loop(0, PARTS, chunk, 0)

        run_pairs_singly(list_ref, visit)
        slots = top_ref[0:rows]
        top = slots.max(1, keepdims=True)
        total = (sum_ref[0:rows] * jnp.exp(slots - top)).sum(1)
        store_blocks(out_ref, log_or_lowest(total, top[:, 0] + shift))


def tgt_sums(
    potential, reach, list_ref, held_ref, tall_ref, src_ref, weight_ref, sum_ref, top_ref, out_ref
):
    rows, cols = src_ref.shape[1] // BLOCK, tall_ref.shape[0] // BLOCK
    weights, shift, safe = factors(potential, reach)
    weight_ref[...] = weights
    sum_ref[...] = jnp.zeros_like(sum_ref)

    def store(block, total, top):
        values = log_or_lowest(total, top)
        for part in range(PARTS):
            at = block * PARTS + part
            out_ref[0, at : at + 1, :] = lane_part(values, part)

    @pl.when(safe)
    def _():
        def visit(index, pair):
            src_block, tgt_block = place(pair, rows, cols)
            at = jnp.where(pair < rows * cols, tgt_block, cols)
            tile = jnp.exp(tile_of(tall_ref, src_ref, src_block, tgt_block))
            sum_ref[at] += fold_lanes(tile * weight_ref[pl.ds(src_block, 1), :], jnp.add)

        def visit_held(index, pair):
            src_block, tgt_block = place(pair, rows, cols)
            at = jnp.where(pair < rows * cols, tgt_block, cols)
            slot = jnp.minimum(index, HELD)
            right = weight_ref[pl.ds(src_block, 1), :]
            for start in range(0, BLOCK, HELD_ROWS):
                tile = held_ref[slot, start : start + HELD_ROWS, :] * right
                sum_ref[at, start : start + HELD_ROWS, :] += fold_lanes(tile, jnp.add)

        held = held_of(list_ref)
        run_pairs(list_ref, 0, held, HELD_GROUP, visit_held)
        run_pairs(list_ref, held, count_of(list_ref), GROUP, visit)
        for block in range(cols):
            store(block, sum_ref[block].T.sum(0, keepdims=True), shift)

    @pl.when(jnp.logical_not(safe))
    def _():
        top_ref[...] = jnp.full_like(top_ref, LOWEST)

        def visit(pair):
            src_block, tgt_block = place(pair, rows, cols)
            right = weight_ref[pl.ds(src_block, 1), :]

            def chunk(index, carry):
                start = pl.multiple_of(index * LANES, LANES)
                tile = tile_of(tall_ref, src_ref, src_block, tgt_block, start, LANES) + right
                at = (tgt_block, pl.ds(start, LANES), slice(None))
                old = top_ref[at]
                new = jnp.maximum(old, fold_lanes(tile, jnp.maximum))
                more = fold_lanes(jnp.exp(tile - jnp.concatenate([new] * PARTS, axis=1)), jnp.add)
                sum_ref[at] = sum_ref[at] * jnp.exp(old - new) + more
                top_ref[at] = new
                return carry

            lax.fori_loop(0, PARTS, chunk, 0)

        run_pairs_singly(list_ref, visit)
        for block in range(cols):
            slots = top_ref[block].T
            top = slots.max(0, keepdims=True)
            total = (sum_ref[block].T * jnp.exp(slots - top)).sum(0, keepdims=True)
            store(block, total, top + shift)

    for copy in range(1, out_ref.shape[0]):
        out_ref[copy] = out_ref[0]


def store_squares(cells_ref, out_ref, first, count):
    for block in range(first, first + count):
        cells = cells_ref[:, block * BLOCK : (block + 1) * BLOCK].astype(jnp.float32)
        squares = jnp.sum(cells * cells, axis=0, keepdims=True)
        for part in range(PARTS):
            at = block * PARTS + part
            out_ref[at : at + 1, :] = lane_part(squares, part)


def first_src_kernel(
    pattern_hbm, src_hbm, tgt_hbm, pot_hbm, room_ref,
    out_ref, src_ref, src_sq_ref, tgt_sq_ref, reach_ref, tall_ref, list_ref, held_ref,
    pattern_ref, tgt_ref, pot_ref, sems, spread_ref, sum_ref, top_ref,
):
    tgt_copy, pattern_copy, pot_copy = copies = [
        pltpu.make_async_copy(source, target, sems.at[at])
        for at, (source, target) in enumerate(
            [(tgt_hbm, tgt_ref), (pattern_hbm, pattern_ref), (pot_hbm, pot_ref)]
        )
    ]
    width = src_ref.shape[1] // CHUNKS
    src_copies = []
    for chunk in range(CHUNKS):
        lanes = pl.ds(chunk * width, width)
        src_copies.append(
            pltpu.make_async_copy(src_hbm.at[:, lanes], src_ref.at[:, lanes], sems.at[3 + chunk])
        )
    for copy in copies + src_copies:
        copy.start()
    tgt_copy.wait()
    pattern_copy.wait()
    list_pairs(pattern_ref, list_ref)
    for block in range(tgt_ref.shape[1] // BLOCK):
        cells = tgt_ref[:, block * BLOCK : (block + 1) * BLOCK].astype(jnp.float32) * 4.0
        tall_ref[block * BLOCK : (block + 1) * BLOCK, :] = cells.T.astype(jnp.bfloat16)
    store_squares(tgt_ref, tgt_sq_ref, 0, tgt_ref.shape[1] // BLOCK)
    pot_copy.wait()
    for copy in src_copies:
        copy.wait()
    store_squares(src_ref, src_sq_ref, 0, src_ref.shape[1] // BLOCK)
    reach = 4.0 * jnp.sqrt(jnp.max(src_sq_ref[...], keepdims=True)) * jnp.sqrt(
        jnp.max(tgt_sq_ref[...], keepdims=True)
    )
    reach_ref[...] = jnp.broadcast_to(reach, reach_ref.shape)
    potential = 2.0 * (pot_ref[...] - tgt_sq_ref[...])
    src_sums(
        potential, reach, True, list_ref, held_ref, tall_ref, src_ref, spread_ref, sum_ref,
        top_ref, out_ref,
    )


def src_kernel(
    list_ref, held_ref, src_ref, tall_ref, gathered_ref, mass_ref, reach_ref,
    out_ref,
    spread_ref, sum_ref, top_ref,
):
    gathered = gathered_ref[...]
    top = gathered.max(0)
    potential = mass_ref[...] - (top + jnp.log(jnp.exp(gathered - top[None]).sum(0)))
    src_sums(
        potential, reach_ref[0:1, 0:1], False, list_ref, held_ref, tall_ref, src_ref, spread_ref,
        sum_ref, top_ref, out_ref,
    )


def tgt_kernel(
    list_ref, held_ref, src_ref, tall_ref, logs_ref, mass_ref, reach_ref,
    out_ref,
    weight_ref, sum_ref, top_ref,
):
    potential = blocks_of(mass_ref) - blocks_of(logs_ref)
    tgt_sums(
        potential, reach_ref[0:1, 0:1], list_ref, held_ref, tall_ref, src_ref, weight_ref, sum_ref,
        top_ref, out_ref,
    )


def last_tgt_kernel(
    list_ref, held_ref, src_ref, tall_ref, logs_ref, mass_ref, reach_ref, src_sq_ref,
    out_ref, src_pot_hbm,
    weight_ref, sum_ref, top_ref, src_pot_ref, sem,
):
    src_pot_ref[...] = src_sq_ref[...] + ENTROPY * (mass_ref[...] - logs_ref[...])
    copy = pltpu.make_async_copy(src_pot_ref, src_pot_hbm, sem)
    copy.start()
    tgt_kernel(
        list_ref, held_ref, src_ref, tall_ref, logs_ref, mass_ref, reach_ref, out_ref, weight_ref,
        sum_ref, top_ref,
    )
    copy.wait()


def call(kernel, args, in_spaces, outs, out_spaces, scratch, name, limit=VMEM_LIMIT, aliases={}):
    return pl.pallas_call(
        kernel,
        out_shape=outs,
        in_specs=[pl.BlockSpec(memory_space=space) for space in in_spaces],
        out_specs=[pl.BlockSpec(memory_space=space) for space in out_spaces],
        scratch_shapes=scratch,
        compiler_params=pltpu.CompilerParams(vmem_limit_bytes=limit),
        name=name,
        input_output_aliases=aliases,
    )(*args)


def floats(*shape):
    return jax.ShapeDtypeStruct(shape, jnp.float32)


def merge_two_kernel(one_ref, other_ref, out_ref):
    one, other = one_ref[...], other_ref[...]
    out_ref[...] = jnp.maximum(one, other) + jnp.log(1.0 + jnp.exp(-jnp.abs(one - other)))


def merge_kernel(own_ref, one_ref, two_ref, three_ref, out_ref):
    own, one, two, three = own_ref[...], one_ref[...], two_ref[...], three_ref[...]
    top = jnp.maximum(jnp.maximum(own, one), jnp.maximum(two, three))
    near = jnp.exp(own - top) + jnp.exp(one - top)
    far = jnp.exp(two - top) + jnp.exp(three - top)
    out_ref[...] = top + jnp.log(near + far)


def over_tgt(logs):
    size = lax.axis_size("tgt")

    def from_peer(values, mask):
        return lax.ppermute(values, "tgt", [(at, at ^ mask) for at in range(size)])

    (logs,) = call(
        merge_two_kernel, [logs, from_peer(logs, 1)], [pltpu.VMEM] * 2, [floats(*logs.shape)],
        [pltpu.VMEM], [], "merge_two", MERGE_LIMIT,
    )
    for stage in (2, 8):
        peers = [from_peer(logs, stage * mask) for mask in (1, 2, 3)]
        (logs,) = call(
            merge_kernel, [logs] + peers, [pltpu.VMEM] * 4, [floats(*logs.shape)], [pltpu.VMEM], [],
            "merge", MERGE_LIMIT,
        )
    return logs


def local(src_cells, tgt_cells, src_logmass, tgt_logmass, init_potential, pattern):
    copies = lax.axis_size("src")
    depth, src_count = src_cells.shape
    tgt_count = tgt_cells.shape[1]
    rows, cols = pattern.shape
    src_shape = (src_count // LANES, LANES)
    tgt_shape = (tgt_count // LANES, LANES)
    src_mass = src_logmass.reshape(src_shape)
    tgt_mass = tgt_logmass.reshape(tgt_shape)
    vmem, smem, hbm = pltpu.VMEM, pltpu.SMEM, pltpu.HBM

    src_scratch = [
        vmem((tgt_count, LANES), jnp.float32),
        vmem((rows + 1, 8, BLOCK), jnp.float32),
        vmem((rows + 1, 8, BLOCK), jnp.float32),
    ]
    tgt_scratch = [
        vmem((rows, BLOCK), jnp.float32),
        vmem((cols + 1, BLOCK, LANES), jnp.float32),
        vmem((cols + 1, BLOCK, LANES), jnp.float32),
    ]
    (room,) = call(
        lambda room_ref: None, [], [], [vmem((HELD + 1, BLOCK, BLOCK), jnp.float32)], [vmem], [], "room",
        MERGE_LIMIT,
    )
    logs, src_kept, src_sq, tgt_sq, reach, tall, pairs, held = call(
        first_src_kernel,
        [
            pltpu.with_memory_space_constraint(array, hbm)
            for array in (pattern.T, src_cells, tgt_cells, init_potential.reshape(tgt_shape))
        ]
        + [pltpu.with_memory_space_constraint(room, vmem)],
        [hbm] * 4 + [vmem],
        [
            floats(*src_shape), jax.ShapeDtypeStruct(src_cells.shape, src_cells.dtype),
            floats(*src_shape), floats(*tgt_shape), floats(8, LANES),
            jax.ShapeDtypeStruct((tgt_count, depth), jnp.bfloat16),
            jax.ShapeDtypeStruct((rows * cols + GROUP + 2,), jnp.int32),
            vmem((HELD + 1, BLOCK, BLOCK), jnp.float32),
        ],
        [vmem] * 6 + [smem, vmem],
        [
            smem((cols, rows), jnp.int32), vmem(tgt_cells.shape, tgt_cells.dtype),
            vmem(tgt_shape, jnp.float32), pltpu.SemaphoreType.DMA((3 + CHUNKS,)),
        ] + src_scratch,
        "src_first", aliases={4: 7},
    )
    held = pltpu.with_memory_space_constraint(held, vmem)
    for sweep in range(SWEEPS):
        if sweep:
            (logs,) = call(
                src_kernel, [pairs, held, src_kept, tall, gathered, tgt_mass, reach], [smem] + [vmem] * 6,
                [floats(*src_shape)], [vmem], src_scratch, "src_next",
            )
        logs = over_tgt(logs)
        args = [pairs, held, src_kept, tall, logs, src_mass, reach]
        if sweep < SWEEPS - 1:
            (logs,) = call(
                tgt_kernel, args, [smem] + [vmem] * 6, [floats(copies, *tgt_shape)], [vmem],
                tgt_scratch, "tgt",
            )
        else:
            logs, src_pot = call(
                last_tgt_kernel, args + [src_sq], [smem] + [vmem] * 7,
                [floats(copies, *tgt_shape), floats(*src_shape)], [vmem, hbm],
                tgt_scratch + [vmem(src_shape, jnp.float32), pltpu.SemaphoreType.DMA], "tgt_last",
            )
        gathered = lax.all_to_all(logs, "src", 0, 0)
    top = gathered.max(0)
    tgt_logs = top + jnp.log(jnp.exp(gathered - top[None]).sum(0))
    tgt_pot = tgt_sq + ENTROPY * (tgt_mass - tgt_logs)
    return src_pot.reshape(-1), tgt_pot.reshape(-1)


def solution(mesh):
    return jax.shard_map(
        local,
        mesh=mesh,
        in_specs=(P(None, "src"), P(None, "tgt"), P("src"), P("tgt"), P("tgt"), P("src", "tgt")),
        out_specs=(P("src"), P("tgt")),
        check_vma=False,
    )
```
